32 devices in a mesh: sec: 4 (over z), row: 4 (over x, core), col: 2 (over y).
Axes of the slice: x: 2, y: 2, z: 4, core: 2. Of those that a mesh axis runs over, the one named last changes fastest.
Arguments:
- vel_modes: float32 [3, 2, 4, 1024, 1024], P(None, None, 'sec', 'row', 'col'), may hold values from -0.005859375 to 0.005859375
- scalar: float32 [4, 2048, 2048], P('sec', 'row', 'col'), may hold values from -6 to 6
- obstacle: int32 [4, 16, 16], P('sec', 'row', 'col'), may hold values from 0 to 2
Outputs:
- scalar_next: float32 [4, 2048, 2048], P('sec', 'row', 'col')
The draws below stay inside these ranges and needn't reach their ends.
All inputs are finite; a program needn't handle non-finite values.
Results may differ from the reference program's by a relative error of at most 0.00005.
Values sent between devices are 32-bit elements; how exact they have to be, the bound alone decides.
No kernel may reach another device: no remote copies, remote signals or barrier semaphores. Data moves between devices by JAX's collectives and lax.ppermute only.
A program may use at most 128 MiB of HBM per device.

```python
import jax
import jax.numpy as jnp
from jax import lax

NV = 1024
NS = 2048
BLOCK = 128
PLANES = 4
TILES = 16


def set_ends(array, stream_key, low, top_value):
    longest = array.shape.index(max(array.shape))
    spots = []
    for shift in (0, 1):
        where = [jax.random.randint(jax.random.fold_in(stream_key, axis), (), 0, length) for axis, length in enumerate(array.shape)]
        where[longest] = (where[longest] + shift) % array.shape[longest]
        spots.append(tuple(where))
    return array.at[spots[0]].set(low).at[spots[1]].set(top_value)


def shard_levels(rng, shape, cuts, least, largest):
    factor_of = 1.0
    for axis_at, shards_of in cuts:
        steps = jax.random.uniform(jax.random.fold_in(jax.random.fold_in(rng, 6), axis_at), (shards_of,), jnp.float32, least / len(cuts), largest / len(cuts))
        factor_of = factor_of * jnp.repeat(jnp.exp(steps), shape[axis_at] // shards_of).reshape((-1,) + (1,) * (len(shape) - 1 - axis_at))
    return factor_of


def centred(stream_key, shape, width, bound, pieces=(), kind=jnp.bfloat16):
    result = width * jax.random.normal(stream_key, shape, jnp.float32)
    if pieces:
        result = result * shard_levels(stream_key, shape, pieces, -0.22, 0.18)
    return jnp.clip(result, -bound, bound).astype(kind)


def setup_inputs(seed: int = 0) -> dict:
    key_list = jax.random.split(jax.random.key(seed), 4)
    return {
        "vel_modes": centred(key_list[0], (3, 2, PLANES, NV, NV), (NV * NV) ** -0.5, 0.005859375, ((2, 4), (3, 4), (4, 2)), jnp.float32),
        "scalar": centred(key_list[1], (PLANES, NS, NS), 1.0, 6.0, ((0, 4), (1, 4), (2, 2)), jnp.float32),
        "obstacle": set_ends(jax.random.randint(key_list[2], (PLANES, TILES, TILES), 0, 3), jax.random.fold_in(key_list[2], 1), 0, 2).astype(jnp.int32),
    }


def pad_modes(spectral):
    middle = NV // 2
    filler = jnp.zeros((NS - NV, NV), spectral.dtype)
    spectral = jnp.concatenate([spectral[:middle], filler, spectral[middle:]], 0)
    filler = jnp.zeros((NS, NS - NV), spectral.dtype)
    return jnp.concatenate([spectral[:, :middle], filler, spectral[:, middle:]], 1)


def plane_field(mode_pair):
    spectrum = pad_modes(mode_pair[0] + 1j * mode_pair[1])
    return jnp.real(jnp.fft.ifft2(spectrum)) * (NS * NS)


def reference(vel_modes, scalar, obstacle):
    fields = [lax.map(plane_field, (vel_modes[component, 0], vel_modes[component, 1])) for component in range(3)]
    right_cell = jnp.roll(scalar, -1, 2)
    left_cell = jnp.roll(scalar, 1, 2)
    front_cell = jnp.roll(scalar, -1, 1)
    back_cell = jnp.roll(scalar, 1, 1)
    padded = jnp.pad(scalar, ((1, 1), (0, 0), (0, 0)))
    above_cell = padded[2:]
    below_cell = padded[:-2]
    transport = fields[0] * (right_cell - left_cell) + fields[1] * (front_cell - back_cell) + fields[2] * (above_cell - below_cell)
    laplace = right_cell + left_cell + front_cell + back_cell + above_cell + below_cell - 6.0 * scalar
    cell_flags = jnp.repeat(jnp.repeat(obstacle.astype(jnp.float32), BLOCK, 1), BLOCK, 2)
    return scalar - 0.125 * transport + 0.04 * laplace - 0.25 * cell_flags * (scalar - 1.0)
```

```python
import functools
import math

import jax
import jax.numpy as jnp
from jax import lax
from jax.experimental import pallas as pl
from jax.experimental.pallas import tpu as pltpu
from jax.sharding import PartitionSpec as P

NV = 1024
NS = 2048
BLOCK = 128
CORES = 2
LANES = 128
MIB = 1 << 20

two_pi = 2.0 * math.pi
highest = lax.Precision.HIGHEST
bf16 = jnp.bfloat16
f32 = jnp.float32


def split(value):
    high = value.astype(bf16)
    return high, (value - high.astype(f32)).astype(bf16)


def dot(left, right):
    return jnp.dot(left, right, preferred_element_type=f32)


def dot3(left_high, left_low, right_high, right_low):
    return dot(left_high, right_high) + dot(left_low, right_high) + dot(left_high, right_low)


def cost(flops, bytes_accessed):
    return pl.CostEstimate(flops=int(flops), bytes_accessed=int(bytes_accessed), transcendentals=0)


def padded(array, sides, width, wrap):
    for axis, dim in sides:
        size, length = (lax.axis_size(axis), array.shape[dim])
        up = [(i, (i + 1) % size) for i in range(size if wrap else size - 1)]
        down = [(j, i) for i, j in up]
        last = lax.slice_in_dim(array, length - width, length, axis=dim)
        first = lax.slice_in_dim(array, 0, width, axis=dim)
        before = lax.ppermute(last, axis, up)
        after = lax.ppermute(first, axis, down)
        array = jnp.concatenate([before, array, after], axis=dim)
    return array


def wavenumbers(indices):
    return jnp.where(indices < NV // 2, indices, indices - NV)


def phase_cos_sin(products):
    angles = (products % NS).astype(f32) * (two_pi / NS)
    return jnp.cos(angles), jnp.sin(angles)


def table_kernel(c1, s1, c2, s2, cos_high, cos_low, sin_high, sin_low):
    base_cos, base_sin = c1[...], s1[...]
    for tile in range(c2.shape[1]):
        turn_cos, turn_sin = c2[:, tile : tile + 1], s2[:, tile : tile + 1]
        where = pl.ds(tile * LANES, LANES)
        high, low = split(base_cos * turn_cos - base_sin * turn_sin)
        cos_high[:, where] = high
        cos_low[:, where] = low
        high, low = split(base_sin * turn_cos + base_cos * turn_sin)
        sin_high[:, where] = high
        sin_low[:, where] = low


def phase_table(row_ids, first, count, shift):
    rows = row_ids.shape[0]
    tiles = count // LANES
    near = row_ids[:, None] * (first + jnp.arange(LANES, dtype=jnp.int32))[None] + shift[:, None]
    far = row_ids[:, None] * (jnp.arange(tiles, dtype=jnp.int32) * LANES)[None]
    step = math.gcd(rows, 256)
    return pl.pallas_call(
        table_kernel,
        grid=(rows // step,),
        in_specs=[pl.BlockSpec((step, LANES), lambda i: (i, 0))] * 2
        + [pl.BlockSpec((step, tiles), lambda i: (i, 0))] * 2,
        out_specs=[pl.BlockSpec((step, count), lambda i: (i, 0))] * 4,
        out_shape=[jax.ShapeDtypeStruct((rows, count), bf16)] * 4,
        compiler_params=pltpu.CompilerParams(vmem_limit_bytes=32 * MIB),
        cost_estimate=cost(rows * count * 14, rows * count * 8),
        name="phase_table",
    )(*phase_cos_sin(near), *phase_cos_sin(far))


def merge_kernel(flags, row_ref, col_ref, out_ref):
    rows, cols = out_ref.shape
    from_row, from_col = row_ref[...], col_ref[...]
    upper_home = flags[0] == 1
    plain = jnp.where(upper_home, from_row, from_col)
    mirrored = jnp.where(upper_home, from_col, from_row)

    def flip(size):
        total = lax.broadcasted_iota(jnp.int32, (size, size), 0) + lax.broadcasted_iota(
            jnp.int32, (size, size), 1
        )
        return jnp.where(total == size, 1.0, 0.0).astype(bf16)

    flip_cols, flip_rows = flip(cols), flip(rows)
    high, low = split(mirrored)
    high, low = split(dot(high, flip_cols) + dot(low, flip_cols))
    turned = dot(flip_rows, high) + dot(flip_rows, low)
    out_ref[...] = plain + jnp.where(flags[1] == 1, -turned, turned)


def merge(flags, from_row, from_col):
    rows, cols = from_row.shape
    return pl.pallas_call(
        merge_kernel,
        in_specs=[pl.BlockSpec(memory_space=pltpu.SMEM)]
        + [pl.BlockSpec(memory_space=pltpu.VMEM)] * 2,
        out_specs=pl.BlockSpec(memory_space=pltpu.VMEM),
        out_shape=jax.ShapeDtypeStruct((rows, cols), f32),
        compiler_params=pltpu.CompilerParams(vmem_limit_bytes=32 * MIB),
        cost_estimate=cost(4 * rows * cols * (rows + cols), rows * cols * 12),
        name="merge_modes",
    )(flags, from_row, from_col)


def transform_kernel(layout, *refs):
    count = len(layout)
    pieces = refs[:count]
    xc_high, xc_low, xs_high, xs_low, yc_high, yc_low, ys_high, ys_low = refs[count : count + 8]
    send_ref, keep_ref, modes_high, modes_low = refs[count + 8 :]

    @pl.when(pl.program_id(0) == 0)
    def _():
        for ref, (top, left) in zip(pieces, layout):
            high, low = split(ref[...])
            where = (pl.ds(top, ref.shape[0]), pl.ds(left, ref.shape[1]))
            modes_high[where] = high
            modes_low[where] = low

    high, low = modes_high[...], modes_low[...]
    real_high, real_low = split(dot3(high, low, xc_high[...], xc_low[...]))
    imag_high, imag_low = split(dot3(high, low, xs_high[...], xs_low[...]))
    total = dot3(yc_high[...], yc_low[...], real_high, real_low) - dot3(
        ys_high[...], ys_low[...], imag_high, imag_low
    )
    here = send_ref.shape[0]
    send_ref[...] = total[:here]
    keep_ref[...] = total[here:]


def transform(pieces, layout, x_tables, y_tables):
    depth, x_count = x_tables[0].shape
    y_both, rows = y_tables[0].shape
    tile = math.gcd(x_count, 256)
    whole = lambda shape: pl.BlockSpec(shape, lambda i: (0, 0))
    flops = 6 * (2 * rows * depth * x_count + 2 * y_both * rows * x_count)
    out_spec = pl.BlockSpec((y_both // CORES, tile), lambda i: (0, i))
    return pl.pallas_call(
        functools.partial(transform_kernel, layout),
        grid=(x_count // tile,),
        in_specs=[whole(piece.shape) for piece in pieces]
        + [pl.BlockSpec((depth, tile), lambda i: (0, i))] * 4
        + [whole((y_both, rows))] * 4,
        out_specs=[out_spec] * 2,
        out_shape=[jax.ShapeDtypeStruct((y_both // CORES, x_count), f32)] * 2,
        scratch_shapes=[pltpu.VMEM((rows, depth), bf16)] * 2,
        compiler_params=pltpu.CompilerParams(vmem_limit_bytes=48 * MIB),
        cost_estimate=cost(flops, depth * x_count * 8 + y_both * x_count * 4),
        name="modes_to_velocity",
    )(*pieces, *x_tables, *y_tables)


def ring(array, axis, perm, size):
    arrays = [array]
    for _ in range(size - 1):
        arrays.append(lax.ppermute(arrays[-1], axis, perm))
    return arrays


def body(vel_modes, scalar, obstacle):
    planes_here, y_count, x_count = scalar.shape
    wave_rows, wave_cols = vel_modes.shape[3:]
    row_size, col_size = lax.axis_size("row"), lax.axis_size("col")
    row, col = lax.axis_index("row"), lax.axis_index("col")
    pairs = row_size // (2 * CORES)
    upper = row >= row_size // 2
    right = col >= col_size // 2
    mirror = jnp.where(upper, row_size - 1 - row, row)
    batch = [(part, plane) for part in range(3) for plane in range(planes_here)]

    flip_row = [(i, row_size - 1 - i) for i in range(row_size)]
    flip_col = [(i, col_size - 1 - i) for i in range(col_size)]
    next_col = [(i, (i + 1) % col_size) for i in range(col_size)]
    mates = [(i, i // CORES * CORES + (i + 1) % CORES) for i in range(row_size)]
    lower_ring = [
        (i, (i // CORES + 1) % pairs * CORES + i % CORES) for i in range(row_size // 2)
    ]
    next_pair = lower_ring + [(row_size - 1 - i, row_size - 1 - j) for i, j in lower_ring]

    kind = right.astype(jnp.int32)
    row_modes = lax.dynamic_index_in_dim(vel_modes, kind, 1, keepdims=False)
    col_modes = lax.dynamic_index_in_dim(vel_modes, 1 - kind, 1, keepdims=False)
    flags = jnp.stack([upper.astype(jnp.int32), kind])
    met = [
        (
            lax.ppermute(row_modes[part, plane], "row", flip_row),
            lax.ppermute(col_modes[part, plane], "col", flip_col),
        )
        for part, plane in batch
    ]

    half = wave_rows // 2
    layout = []
    gathered = []
    for from_row, from_col in met:
        own = merge(flags, from_row, from_col)
        flipped = lax.ppermute(own, "row", flip_row)
        across = ring(own, "col", next_col, col_size)
        top = ring(flipped[:half], "col", next_col, col_size)
        bottom = [lax.ppermute(piece[half:], "row", flip_row) for piece in across[1:]]
        pieces = across + [flipped]
        layout = [(0, i * wave_cols) for i in range(col_size + 1)]
        for i in range(1, col_size):
            pieces += [top[i], bottom[i - 1]]
            left = (col_size + i) * wave_cols
            layout += [(0, left), (half, left)]
        gathered.append(list(zip(*[ring(piece, "row", next_pair, pairs) for piece in pieces])))

    ids, shifts = [], []
    within = jnp.arange(wave_cols, dtype=jnp.int32)
    blocks = []
    for flipped_side in (False, True):
        for step in range(col_size):
            home_col = (col - step) % col_size
            home_upper = upper != flipped_side
            block = jnp.where(home_upper, home_col, col_size - 1 - home_col)
            part = (home_col >= col_size // 2).astype(jnp.int32)
            blocks.append((part, block))
            ids.append(wavenumbers(block * wave_cols + within))
            shifts.append(jnp.broadcast_to(part * (NS // 4), (wave_cols,)))
    x_ids, x_shifts = jnp.concatenate(ids), jnp.concatenate(shifts)
    x_tables = phase_table(x_ids, col * x_count, x_count, x_shifts)
    own_cells = row * y_count + jnp.arange(y_count, dtype=jnp.int32)
    mate = row // CORES * CORES + (row + 1) % CORES
    mate_cells = mate * y_count + jnp.arange(y_count, dtype=jnp.int32)
    y_cells = jnp.concatenate([mate_cells, own_cells])
    y_tables = []
    for step in range(pairs):
        rows_block = (mirror // CORES - step) % pairs * CORES + mirror % CORES
        y_tables.append(
            phase_table(y_cells, rows_block * wave_rows, wave_rows, jnp.zeros_like(y_cells))
        )

    edge = jnp.concatenate([vel_modes[:, :, :, 0, :], vel_modes[:, :, :, :, 0]], axis=-1)
    edges = lax.all_gather(edge, ("row", "col"), axis=0)
    edges = edges.reshape(row_size, col_size, 3, 2, planes_here, wave_cols + wave_rows)
    edges = edges[row_size // 2 :]
    edge_rows = edges[..., :wave_cols].transpose(2, 4, 0, 3, 1, 5)
    edge_rows = edge_rows.reshape(3 * planes_here * (row_size // 2), 2, col_size, wave_cols)
    edge_rows = jnp.concatenate(
        [
            lax.dynamic_index_in_dim(
                lax.dynamic_index_in_dim(edge_rows, part, 1, keepdims=False), block, 1, keepdims=False
            )
            for part, block in blocks
        ],
        axis=-1,
    )
    rows_high, rows_low = split(edge_rows)
    shape = (3, planes_here, row_size // 2, x_count)
    row_real = dot3(rows_high, rows_low, x_tables[0], x_tables[1]).reshape(shape)
    row_imag = dot3(rows_high, rows_low, x_tables[2], x_tables[3]).reshape(shape)
    upper_ids = NV // 2 + jnp.arange(NV // 2, dtype=jnp.int32)
    edge_ids = wavenumbers(upper_ids[::wave_rows])
    row_cos, row_sin = phase_cos_sin(own_cells[:, None] * edge_ids[None])

    edge_cols = edges[..., wave_cols:].at[..., 0].set(0.0).transpose(2, 4, 3, 1, 0, 5)
    edge_cols = edge_cols.reshape(3, planes_here, 2, col_size, NV // 2)
    up_cos, up_sin = phase_cos_sin(wavenumbers(upper_ids)[:, None] * own_cells[None])
    cols_cos = jnp.einsum("kprcm,my->kprcy", edge_cols, up_cos, precision=highest)
    cols_sin = jnp.einsum("kprcm,my->kprcy", edge_cols, up_sin, precision=highest)
    col_real = cols_cos[:, :, 0] - cols_sin[:, :, 1]
    col_imag = cols_sin[:, :, 0] + cols_cos[:, :, 1]
    x_cells = col * x_count + jnp.arange(x_count, dtype=jnp.int32)
    first_ids = wavenumbers(jnp.arange(col_size, dtype=jnp.int32) * wave_cols)
    col_cos, col_sin = phase_cos_sin(first_ids[:, None] * x_cells[None])
    whole_shape = (3, planes_here, row_size // 2, y_count)
    left = jnp.concatenate(
        [
            jnp.broadcast_to(row_cos.T, whole_shape),
            jnp.broadcast_to(-row_sin.T, whole_shape),
            col_real,
            -col_imag,
        ],
        axis=2,
    )
    whole_shape = (3, planes_here, col_size, x_count)
    right_side = jnp.concatenate(
        [
            row_real,
            row_imag,
            jnp.broadcast_to(col_cos, whole_shape),
            jnp.broadcast_to(col_sin, whole_shape),
        ],
        axis=2,
    )
    edge_velocity = jnp.einsum("kpey,kpex->kpyx", left, right_side, precision=highest)

    velocity = []
    for index, (part, plane) in enumerate(batch):
        kept = edge_velocity[part, plane]
        sent = None
        for step in range(pairs):
            send, keep = transform(gathered[index][step], layout, x_tables, y_tables[step])
            sent = send if sent is None else sent + send
            kept = kept + keep
        velocity.append(kept + lax.ppermute(sent, "row", mates))
    velocity = jnp.stack(velocity).reshape(3, planes_here, y_count, x_count)

    stacked = padded(scalar, (("sec", 0),), 1, False)
    bordered = padded(scalar, (("row", 1), ("col", 2)), 1, True)
    right_cell = bordered[:, 1:-1, 2:]
    left_cell = bordered[:, 1:-1, :-2]
    front_cell = bordered[:, 2:, 1:-1]
    back_cell = bordered[:, :-2, 1:-1]
    above_cell = stacked[2:]
    below_cell = stacked[:-2]
    transport = (
        velocity[0] * (right_cell - left_cell)
        + velocity[1] * (front_cell - back_cell)
        + velocity[2] * (above_cell - below_cell)
    )
    laplace = (
        right_cell + left_cell + front_cell + back_cell + above_cell + below_cell - 6.0 * scalar
    )
    tile_rows = obstacle.shape[1]
    tile_cols = obstacle.shape[2]
    cell_flags = jnp.broadcast_to(
        obstacle.astype(f32)[:, :, None, :, None],
        (planes_here, tile_rows, BLOCK, tile_cols, BLOCK),
    ).reshape(planes_here, y_count, x_count)
    return scalar - 0.125 * transport + 0.04 * laplace - 0.25 * cell_flags * (scalar - 1.0)


def solution(mesh):
    in_specs = (P(None, None, "sec", "row", "col"), P("sec", "row", "col"), P("sec", "row", "col"))
    out_specs = P("sec", "row", "col")
    return jax.shard_map(body, mesh=mesh, in_specs=in_specs, out_specs=out_specs, check_vma=False)
```

```python
import functools
import math

import jax
import jax.numpy as jnp
from jax import lax
from jax.experimental import pallas as pl
from jax.experimental.pallas import tpu as pltpu
from jax.sharding import PartitionSpec as P

NV = 1024
NS = 2048
BLOCK = 128
CORES = 2
LANES = 128
MIB = 1 << 20
VMEM_MIB = 60

two_pi = 2.0 * math.pi
highest = lax.Precision.HIGHEST
bf16 = jnp.bfloat16
f32 = jnp.float32


def split(value):
    high = value.astype(bf16)
    return high, (value - high.astype(f32)).astype(bf16)


def split_outside(value):
    high = lax.reduce_precision(value, 8, 7)
    return high.astype(bf16), (value - high).astype(bf16)


def dot(left, right):
    return jnp.dot(left, right, preferred_element_type=f32)


def dot3(left_high, left_low, right_high, right_low):
    return dot(left_high, right_high) + dot(left_low, right_high) + dot(left_high, right_low)


def cost(flops, bytes_accessed):
    return pl.CostEstimate(flops=int(flops) >> 8, bytes_accessed=int(bytes_accessed) >> 8, transcendentals=0)


def behind(value, *others):
    return value if not others else lax.optimization_barrier((value, others))[0]


def wavenumbers(indices):
    return jnp.where(indices < NV // 2, indices, indices - NV)


def phase_cos_sin(products):
    quarter = NS // 4
    turns = (products + quarter // 2) >> (quarter.bit_length() - 1)
    angle = (products - turns * quarter).astype(f32) * (two_pi / NS)
    square = angle * angle
    cos = 1.0 + square * (-1 / 2 + square * (1 / 24 + square * (-1 / 720 + square * (1 / 40320))))
    sin = 1.0 + square * (
        -1 / 6 + square * (1 / 120 + square * (-1 / 5040 + square * (1 / 362880)))
    )
    sin = sin * angle
    odd = (turns & 1) == 1
    cos, sin = jnp.where(odd, sin, cos), jnp.where(odd, cos, sin)
    turned = turns & 3
    cos = jnp.where((turned == 1) | (turned == 2), -cos, cos)
    sin = jnp.where(turned >= 2, -sin, sin)
    return cos, sin


def table_kernel(parts, starts, cos_high, cos_low, sin_high, sin_low):
    rows, count = cos_high.shape
    step, steps = pl.program_id(0), pl.num_programs(0) // parts
    first = starts[0] if parts == 1 else jnp.where(step < steps, starts[0], starts[1])
    row_ids = first + lax.rem(step, steps) * rows
    row_ids = row_ids + lax.broadcasted_iota(jnp.int32, (rows, LANES), 0)
    lanes = lax.broadcasted_iota(jnp.int32, (rows, LANES), 1)

    cos, sin = phase_cos_sin(row_ids * (starts[2] + lanes))
    step_cos, step_sin = phase_cos_sin(row_ids * LANES)
    for tile in range(count // LANES):
        where = pl.ds(tile * LANES, LANES)
        cos_high[:, where], cos_low[:, where] = split(cos)
        sin_high[:, where], sin_low[:, where] = split(sin)
        cos, sin = cos * step_cos - sin * step_sin, sin * step_cos + cos * step_sin


def phase_table(row_starts, rows, first, count):
    parts = len(row_starts)
    step = math.gcd(rows, 256)
    starts = jnp.stack([jnp.asarray(x, jnp.int32) for x in (row_starts[0], row_starts[-1], first)])
    return pl.pallas_call(
        functools.partial(table_kernel, parts),
        grid=(parts * rows // step,),
        in_specs=[pl.BlockSpec(memory_space=pltpu.SMEM)],
        out_specs=[pl.BlockSpec((step, count), lambda i: (i, 0))] * 4,
        out_shape=[jax.ShapeDtypeStruct((parts * rows, count), bf16)] * 4,
        compiler_params=pltpu.CompilerParams(vmem_limit_bytes=VMEM_MIB * MIB),
        cost_estimate=cost(rows * count * 14, rows * count * 8),
        name="phase_table",
    )(starts)


def merge_kernel(flags, row_ref, col_ref, out_ref):
    rows, cols = out_ref.shape
    from_row, from_col = row_ref[...], col_ref[...]
    upper_home = flags[0] == 1
    plain = jnp.where(upper_home, from_row, from_col)
    mirrored = jnp.where(upper_home, from_col, from_row)

    def flip(size):
        total = lax.broadcasted_iota(jnp.int32, (size, size), 0) + lax.broadcasted_iota(
            jnp.int32, (size, size), 1
        )
        return jnp.where(total == size, 1.0, 0.0).astype(bf16)

    flip_cols, flip_rows = flip(cols), flip(rows)
    high, low = split(mirrored)
    high, low = split(dot(high, flip_cols) + dot(low, flip_cols))
    turned = dot(flip_rows, high) + dot(flip_rows, low)
    out_ref[...] = plain + jnp.where(flags[1] == 1, -turned, turned)


def merge(flags, from_row, from_col):
    rows, cols = from_row.shape
    return pl.pallas_call(
        merge_kernel,
        grid=(1,),
        in_specs=[pl.BlockSpec(memory_space=pltpu.SMEM)]
        + [pl.BlockSpec((rows, cols), lambda i: (0, 0))] * 2,
        out_specs=pl.BlockSpec((rows, cols), lambda i: (0, 0)),
        out_shape=jax.ShapeDtypeStruct((rows, cols), f32),
        compiler_params=pltpu.CompilerParams(vmem_limit_bytes=VMEM_MIB * MIB),
        cost_estimate=cost(4 * rows * cols * (rows + cols), rows * cols * 12),
        name="merge_modes",
    )(flags, from_row, from_col)


def transform_kernel(layout, groups, first, has_base, finish, *refs):
    count = len(layout)
    pieces, refs = refs[:count], refs[count:]
    (turn_cos, turn_sin, c_high, c_low, s_high, s_low), refs = refs[:6], refs[6:]
    if has_base:
        base, refs = refs[:2], refs[2:]
    if finish:
        (yc_high, yc_low, ys_high, ys_low), refs = refs[:4], refs[4:]
    first_out, second_out, modes_high, modes_low = refs
    rows = modes_high.shape[0] // groups

    @pl.when(pl.program_id(0) == 0)
    def _():
        for ref, (group, top) in zip(pieces, layout):
            high, low = split(ref[...])
            where = pl.ds(group * rows + top, ref.shape[0])
            modes_high[where, :] = high
            modes_low[where, :] = low

    high, low = modes_high[...], modes_low[...]
    part_cos = dot3(high, low, c_high[...], c_low[...])
    part_sin = dot3(high, low, s_high[...], s_low[...])
    real, imag = (base[0][...], base[1][...]) if has_base else (None, None)
    for group in range(groups):
        where = slice(group * rows, (group + 1) * rows)
        p = turn_cos[first + group : first + group + 1, :]
        q = turn_sin[first + group : first + group + 1, :]
        more_real = p * part_cos[where] - q * part_sin[where]
        more_imag = p * part_sin[where] + q * part_cos[where]
        real = more_real if real is None else real + more_real
        imag = more_imag if imag is None else imag + more_imag
    if not finish:
        first_out[...] = real
        second_out[...] = imag
        return
    real_high, real_low = split(real)
    imag_high, imag_low = split(imag)
    total = dot3(yc_high[...], yc_low[...], real_high, real_low) - dot3(
        ys_high[...], ys_low[...], imag_high, imag_low
    )
    here = first_out.shape[0]
    first_out[...] = total[:here]
    second_out[...] = total[here:]


def transform(pieces, layout, first, turns, x_tables, y_tables=None, base=None):
    depth, x_count = x_tables[0].shape
    groups = 1 + max(group for group, _ in layout)
    rows = max(top + piece.shape[0] for piece, (_, top) in zip(pieces, layout))
    finish = y_tables is not None
    tile = math.gcd(x_count, 256)
    whole = lambda shape: pl.BlockSpec(shape, lambda i: (0, 0))
    columns = lambda height: pl.BlockSpec((height, tile), lambda i: (0, i))
    flops = 12 * groups * rows * depth * x_count
    out_rows = rows
    operands = [*pieces, *turns, *x_tables]
    specs = [whole(piece.shape) for piece in pieces]
    specs += [columns(turns[0].shape[0])] * 2 + [columns(depth)] * 4
    if base is not None:
        operands += base
        specs += [columns(rows)] * 2
    if finish:
        y_both = y_tables[0].shape[0]
        out_rows = y_both // CORES
        flops += 12 * y_both * rows * x_count
        operands += y_tables
        specs += [whole((y_both, rows))] * 4
    return pl.pallas_call(
        functools.partial(
            transform_kernel, layout, groups, first, base is not None, finish
        ),
        grid=(x_count // tile,),
        in_specs=specs,
        out_specs=[columns(out_rows)] * 2,
        out_shape=[jax.ShapeDtypeStruct((out_rows, x_count), f32)] * 2,
        scratch_shapes=[pltpu.VMEM((groups * rows, depth), bf16)] * 2,
        compiler_params=pltpu.CompilerParams(vmem_limit_bytes=VMEM_MIB * MIB),
        cost_estimate=cost(flops, 12 * MIB),
        name="modes_to_velocity" if finish else "modes_along_x",
    )(*operands)


def stencil_kernel(sign, *refs):
    (centre, before, following, top, bottom, left_edge, right_edge, above, below, flag) = refs[:10]
    velocity = (refs[10:12], refs[12:14], ())
    edge_left, edge_right = refs[14:16]
    acc_out, dz_out = refs[-2:]
    step, steps = pl.program_id(0), pl.num_programs(0)
    s = centre[...]
    rows, cols = s.shape
    row_at = lax.broadcasted_iota(jnp.int32, s.shape, 0)
    col_at = lax.broadcasted_iota(jnp.int32, s.shape, 1)
    back_row = jnp.where(step == 0, top[...], before[before.shape[0] - 1 :, :])
    front_row = jnp.where(step == steps - 1, bottom[...], following[:1, :])
    back = jnp.where(row_at == 0, back_row, pltpu.roll(s, 1, 0))
    front = jnp.where(row_at == rows - 1, front_row, pltpu.roll(s, rows - 1, 0))
    upright = lambda line: jnp.broadcast_to(line, (8, rows)).T[:, :1]
    left = jnp.where(col_at == 0, upright(left_edge[...]), pltpu.roll(s, 1, 1))
    right = jnp.where(col_at == cols - 1, upright(right_edge[...]), pltpu.roll(s, cols - 1, 1))
    up, down = above[...], below[...]
    lap = right + left + front + back + up + down - 6.0 * s
    dz = sign[0].astype(f32) * (up - down)
    transport = None
    for part, diff in enumerate((right - left, front - back, dz)):
        lhs_high, lhs_low = split(edge_left[part].T)
        rhs_high, rhs_low = split(edge_right[part])
        speed = dot3(lhs_high, lhs_low, rhs_high, rhs_low)
        for ref in velocity[part]:
            speed = speed + ref[...]
        transport = speed * diff if transport is None else transport + speed * diff
    acc_out[...] = s - 0.125 * transport + 0.04 * lap - 0.25 * flag[0] * (s - 1.0)
    dz_out[...] = -0.125 * dz


def stencil(sign, scalar, halos, planes, flag_rows, velocity, edges):
    y_count, x_count = scalar.shape
    top, bottom, left_edge, right_edge = halos
    step = BLOCK
    near = 8
    per_step, last = step // near, y_count // near - 1
    rows = pl.BlockSpec((step, x_count), lambda i: (i, 0))
    row = pl.BlockSpec((1, x_count), lambda i: (0, 0))
    column = pl.BlockSpec((1, step), lambda i: (0, i))
    count = edges[0].shape[1]
    return pl.pallas_call(
        stencil_kernel,
        grid=(y_count // step,),
        in_specs=[
            pl.BlockSpec(memory_space=pltpu.SMEM),
            rows,
            pl.BlockSpec((near, x_count), lambda i: (jnp.maximum(i * per_step - 1, 0), 0)),
            pl.BlockSpec((near, x_count), lambda i: (jnp.minimum((i + 1) * per_step, last), 0)),
            row,
            row,
            column,
            column,
            rows,
            rows,
            pl.BlockSpec((1, 1, x_count), lambda i: (i, 0, 0)),
            rows,
            rows,
            rows,
            rows,
            pl.BlockSpec((3, count, step), lambda i: (0, 0, i)),
            pl.BlockSpec((3, count, x_count), lambda i: (0, 0, 0)),
        ],
        out_specs=[rows] * 2,
        out_shape=[jax.ShapeDtypeStruct((y_count, x_count), f32)] * 2,
        compiler_params=pltpu.CompilerParams(vmem_limit_bytes=VMEM_MIB * MIB),
        cost_estimate=cost(30 * y_count * x_count, 40 * y_count * x_count),
        name="stencil",
    )(sign, scalar, scalar, scalar, top, bottom, left_edge, right_edge, *planes, flag_rows, *velocity, *edges)


def ring(array, axis, perm, size):
    arrays = [array]
    for _ in range(size - 1):
        arrays.append(lax.ppermute(arrays[-1], axis, perm))
    return arrays


def edge_factors(edge_rows, edge_cols, x_tables, own_cells, x_cells, y_first):
    upper_rows, col_size, _, _, planes_here, _ = edge_rows.shape
    wave_rows, wave_cols = NV // 2 // upper_rows, NV // col_size
    y_count, x_count = own_cells.shape[0], x_cells.shape[0]
    kept = edge_rows.transpose(2, 4, 0, 3, 1, 5)
    lead = (3, planes_here, upper_rows, 2, col_size)
    high, low = split_outside(kept.reshape(-1, wave_cols))
    part_cos = dot3(high, low, x_tables[0], x_tables[1]).reshape(lead + (x_count,))
    part_sin = dot3(high, low, x_tables[2], x_tables[3]).reshape(lead + (x_count,))
    real = part_cos[:, :, :, 0] - part_sin[:, :, :, 1]
    imag = part_sin[:, :, :, 0] + part_cos[:, :, :, 1]
    block_ids = wavenumbers(jnp.arange(col_size, dtype=jnp.int32) * wave_cols)
    turn_cos, turn_sin = phase_cos_sin(block_ids[:, None] * x_cells[None])
    row_real = jnp.sum(turn_cos * real - turn_sin * imag, axis=3)
    row_imag = jnp.sum(turn_cos * imag + turn_sin * real, axis=3)
    upper_ids = wavenumbers(NV // 2 + jnp.arange(NV // 2, dtype=jnp.int32))
    row_cos, row_sin = phase_cos_sin(upper_ids[::wave_rows, None] * own_cells[None])

    kept = edge_cols.at[..., 0].set(0.0).transpose(2, 4, 3, 1, 0, 5)
    high, low = split_outside(kept.reshape(-1, NV // 2))
    y_tables = phase_table([-NV // 2], NV // 2, y_first, y_count)
    lead = (3, planes_here, 2, col_size, y_count)
    part_cos = dot3(high, low, y_tables[0], y_tables[1]).reshape(lead)
    part_sin = dot3(high, low, y_tables[2], y_tables[3]).reshape(lead)
    col_real = part_cos[:, :, 0] - part_sin[:, :, 1]
    col_imag = part_sin[:, :, 0] + part_cos[:, :, 1]

    spread = lambda array: jnp.broadcast_to(array, (3, planes_here) + array.shape)
    left = jnp.concatenate([spread(row_cos), spread(-row_sin), col_real, -col_imag], axis=2)
    right = jnp.concatenate([row_real, row_imag, spread(turn_cos), spread(turn_sin)], axis=2)
    return left, right


def body(vel_modes, scalar, obstacle):
    planes_here, y_count, x_count = scalar.shape
    wave_rows, wave_cols = vel_modes.shape[3:]
    row_size, col_size = lax.axis_size("row"), lax.axis_size("col")
    row, col = lax.axis_index("row"), lax.axis_index("col")
    pairs = row_size // (2 * CORES)
    upper = row >= row_size // 2
    right = col >= col_size // 2
    mirror = jnp.where(upper, row_size - 1 - row, row)
    batch = [(part, plane) for part in range(3) for plane in range(planes_here)]

    count = len(batch)

    flip_row = [(i, row_size - 1 - i) for i in range(row_size)]
    flip_col = [(i, col_size - 1 - i) for i in range(col_size)]
    next_col = [(i, (i + 1) % col_size) for i in range(col_size)]
    mates = [(i, i // CORES * CORES + (i + 1) % CORES) for i in range(row_size)]
    lower_ring = [
        (i, (i // CORES + 1) % pairs * CORES + i % CORES) for i in range(row_size // 2)
    ]
    next_pair = lower_ring + [(row_size - 1 - i, row_size - 1 - j) for i, j in lower_ring]

    kind = right.astype(jnp.int32)
    flags = jnp.stack([upper.astype(jnp.int32), kind])
    half = wave_rows // 2

    def choose(index, *after):
        part, plane = batch[index]
        modes, which = vel_modes[part, :, plane], behind(kind, *after)
        row_modes = lax.dynamic_index_in_dim(modes, which, 0, keepdims=False)
        col_modes = lax.dynamic_index_in_dim(modes, 1 - which, 0, keepdims=False)
        return row_modes, col_modes

    def meet(chosen, *after):
        row_modes, col_modes = (behind(array, *after) for array in chosen)
        return lax.ppermute(row_modes, "row", flip_row), lax.ppermute(col_modes, "col", flip_col)

    def spread(met, *after):
        own = merge(behind(flags, *after), *met)
        return ring(own, "col", next_col, col_size), lax.ppermute(own, "row", flip_row)

    def relay(index, across, flipped):
        if index < count // 3:
            return [lax.ppermute(piece, "row", flip_row) for piece in across[1:]]
        if index < 2 * (count // 3):
            return ring(flipped, "col", next_col, col_size)[1:]
        top = ring(flipped[:half], "col", next_col, col_size)[1:]
        bottom = [lax.ppermute(piece[half:], "row", flip_row) for piece in across[1:]]
        return [piece for both in zip(top, bottom) for piece in both]

    near_layout = [(group, 0) for group in range(col_size + 1)]
    split_layout = [(group, top) for group in range(col_size - 1) for top in (0, half)]
    whole_layout = [(group, 0) for group in range(col_size - 1)]

    last = count - planes_here
    spreads, relays, sent, kept = [], [], [], []
    first = choose(0)
    met = [meet(first)]

    late_modes, late_scalar = behind(vel_modes, *first), behind(scalar, *first)
    lines = lambda *arrays: jnp.concatenate([array.reshape(-1, LANES) for array in arrays])
    edge_row, edge_col = late_modes[:, :, :, 0, :], late_modes[:, :, :, :, 0]
    message = lines(edge_row, edge_col, late_scalar[:, 0], late_scalar[:, -1])
    second = choose(1, message)
    met.append(meet(second))
    over = lambda i: i + 1 if i % CORES == CORES - 1 else i - 1
    across = [(i, over(i) % row_size) for i in range(row_size)]
    from_across = lax.ppermute(message, "row", across)

    x_first, y_first = col * x_count, row * y_count
    x_cells = x_first + jnp.arange(x_count, dtype=jnp.int32)
    own_cells = y_first + jnp.arange(y_count, dtype=jnp.int32)
    x_tables = phase_table([0], wave_cols, behind(x_first, *second), x_count)
    base_ids, base_shifts = [], []
    for flipped_side in (False, True):
        for step in range(col_size):
            home_col = (col - step) % col_size
            home_upper = upper != flipped_side
            block = jnp.where(home_upper, home_col, col_size - 1 - home_col)
            base_ids.append(wavenumbers(block * wave_cols))
            base_shifts.append((home_col >= col_size // 2).astype(jnp.int32) * (NS // 4))
    base_ids, base_shifts = jnp.stack(base_ids), jnp.stack(base_shifts)
    turns = phase_cos_sin(base_ids[:, None] * x_cells[None] + base_shifts[:, None])

    def gather(index, *after):
        spreads.append(spread(met[index], *after))

    def pass_on(index, *after):
        across, flipped = spreads[index]
        relays.append(relay(index, [behind(x, *after) for x in across], behind(flipped, *after)))

    gather(0, x_tables[0])
    pass_on(0)

    from_across = behind(from_across, spreads[0][0][0])
    stack, owners = message[None], [list(range(row_size))]
    for stage in range(row_size // CORES):
        perm = across if stage % CORES == 0 else mates
        new = from_across[None] if stage == 0 else lax.ppermute(stack, "row", perm)
        stack = jnp.concatenate([stack, new])
        owners += [[known[sender] for sender, _ in sorted(perm, key=lambda p: p[1])] for known in owners]
    edge_end = (edge_row.size + edge_col.size) // LANES
    side_lines = planes_here * x_count // LANES
    firsts, lasts = stack[:, edge_end : edge_end + side_lines], stack[:, edge_end + side_lines :]
    last_core = row % CORES == CORES - 1
    tops = jnp.where(last_core, lasts[2], lasts[1]).reshape(planes_here, 1, x_count)
    bottoms = jnp.where(last_core, firsts[1], firsts[2]).reshape(planes_here, 1, x_count)
    upper_messages = []
    for place in range(row_size // 2, row_size):
        found = stack[0, :edge_end]
        for item in range(1, stack.shape[0]):
            here = jnp.array([owner == place for owner in owners[item]])[row]
            found = jnp.where(here, stack[item, :edge_end], found)
        upper_messages.append(found)
    message = lines(jnp.stack(upper_messages), late_scalar[:, :, 0], late_scalar[:, :, -1])
    messages = ring(message, "col", next_col, col_size)
    upper_end, side_lines = edge_end * (row_size // 2), planes_here * y_count // LANES
    lefts = messages[1][upper_end + side_lines :].reshape(planes_here, 1, y_count)
    rights = messages[-1][upper_end : upper_end + side_lines].reshape(planes_here, 1, y_count)
    upper_messages = jnp.stack(
        [
            lax.dynamic_index_in_dim(
                jnp.stack(messages), (col - place) % col_size, 0, keepdims=False
            )[:upper_end].reshape(row_size // 2, edge_end, LANES)
            for place in range(col_size)
        ],
        axis=1,
    )

    core = row % CORES
    rows_of = lambda level, i, by: ((level + by) * row_size + i, level * row_size + i)
    one_way, other_way = [], []
    for level in range(lax.axis_size("sec") - 1):
        for i in range(row_size):
            high, low = rows_of(level, i, 1)
            (one_way if i % CORES == 0 else other_way).append((low, high))
            (other_way if i % CORES == 0 else one_way).append((high, low))
    ones = jnp.where(core == 0, scalar[-1:], scalar[:1]) if planes_here > 1 else scalar
    others = jnp.where(core == 0, scalar[:1], scalar[-1:]) if planes_here > 1 else scalar

    mate_first = (row + (row + 1) % CORES - row % CORES) * y_count
    mate_first = behind(mate_first, spreads[0][0][0])
    y_tables = []
    for step in range(pairs):
        rows_block = (mirror // CORES - step) % pairs * CORES + mirror % CORES
        y_tables.append(
            phase_table([mate_first, y_first], y_count, rows_block * wave_rows, wave_rows)
        )
    gather(1, y_tables[-1][0], stack)
    pass_on(1)
    plane_one = lax.ppermute(behind(ones, spreads[1][0][0]), ("sec", "row"), one_way)

    row_end = edge_row.size // LANES
    lead = (row_size // 2, col_size, 3, 2, planes_here)
    edge_rows = upper_messages[:, :, :row_end].reshape(lead + (wave_cols,))
    edge_cols = upper_messages[:, :, row_end:].reshape(lead + (wave_rows,))
    late = behind(y_first, spreads[1][0][0])
    edge_left, edge_right = edge_factors(edge_rows, edge_cols, x_tables, late + jnp.arange(y_count, dtype=jnp.int32), x_cells, late)
    flag_rows = jnp.repeat(obstacle.astype(f32), BLOCK, axis=2)[:, :, None]

    turns = list(turns)

    def near_part(index, *after):
        across, flipped = spreads[index]
        here = ring_all(across + [flipped])
        turned = [behind(turns[0], *after), turns[1]]
        return [transform(pieces, near_layout, 0, turned, x_tables) for pieces in here]

    def far_part(index, bases, *after):
        send = keep = None
        turned = [behind(turns[0], *after), turns[1]]
        for step, pieces in enumerate(ring_all(relays[index])):
            far_layout = whole_layout if len(pieces) == len(whole_layout) else split_layout
            pair = transform(
                pieces, far_layout, col_size + 1, turned, x_tables, y_tables[step], bases[step]
            )
            send = pair[0] if send is None else send + pair[0]
            keep = pair[1] if keep is None else keep + pair[1]
        kept.append(keep)
        sent.append(lax.ppermute(send, "row", mates))

    def ring_all(pieces):
        return list(zip(*[ring(piece, "row", next_pair, pairs) for piece in pieces]))

    flat = lambda groups: [array for group in groups for array in group]
    arrived = lambda index: (*spreads[index][0][1:], spreads[index][1])
    chosen = [first, second]
    bases = []
    for index in range(2, count):
        chosen.append(choose(index, *arrived(index - 2)))
        met.append(meet(chosen[index]))
        if index == 2:
            bases.append(near_part(0, spreads[1][0][0], *chosen[2]))
        bases.append(near_part(index - 1, *flat(bases[-1])))
        gather(index, *flat(bases[-1]), *relays[index - 2], *relays[index - 1])
        if index == 2:
            others = behind(others, plane_one, spreads[index][0][0])
            plane_two = lax.ppermute(others, ("sec", "row"), other_way)
        far_part(index - 2, bases[index - 2], spreads[index][0][0])
        pass_on(index, kept[-1])
    sides = (edge_left, edge_right, lefts, rights, tops, bottoms, flag_rows)
    first_turn, sides = lax.optimization_barrier((turns[0], sides))
    turns[0] = first_turn
    edge_left, edge_right, lefts, rights, tops, bottoms, flag_rows = sides
    far_part(count - 2, bases[-1], kept[-1], plane_two)
    bases.append(near_part(count - 1, kept[-1]))
    far_part(count - 1, bases[-1])

    sign = 1 - 2 * core
    if planes_here > 1:
        plane_one, plane_two = (
            jnp.where(core == 0, plane_one, plane_two),
            jnp.where(core == 0, plane_two, plane_one),
        )
        sign = jnp.ones_like(sign)
    results = []
    for plane in range(planes_here):
        below = plane_one[0] if plane == 0 else scalar[plane - 1]
        above = plane_two[0] if plane == planes_here - 1 else scalar[plane + 1]
        at = [part * planes_here + plane for part in range(3)]
        acc, factor = stencil(
            sign.reshape(1),
            behind(scalar[plane], kept[at[2]]),
            (tops[plane], bottoms[plane], lefts[plane], rights[plane]),
            (above, below),
            flag_rows[plane],
            [kept[at[0]], sent[at[0]], kept[at[1]], sent[at[1]]],
            (edge_left[:, plane], edge_right[:, plane]),
        )
        results.append(acc + (kept[at[2]] + sent[at[2]]) * factor)
    return jnp.stack(results)


def solution(mesh):
    in_specs = (P(None, None, "sec", "row", "col"), P("sec", "row", "col"), P("sec", "row", "col"))
    out_specs = P("sec", "row", "col")
    return jax.shard_map(body, mesh=mesh, in_specs=in_specs, out_specs=out_specs, check_vma=False)
```

```python
import functools
import math

import jax
import jax.numpy as jnp
from jax import lax
from jax.experimental import pallas as pl
from jax.experimental.pallas import tpu as pltpu
from jax.sharding import PartitionSpec as P

NV = 1024
NS = 2048
BLOCK = 128
CORES = 2
LANES = 128
MIB = 1 << 20
VMEM_MIB = 60

two_pi = 2.0 * math.pi
highest = lax.Precision.HIGHEST
bf16 = jnp.bfloat16
f32 = jnp.float32


def split(value):
    high = value.astype(bf16)
    return high, (value - high.astype(f32)).astype(bf16)


def split_outside(value):
    high = lax.reduce_precision(value, 8, 7)
    return high.astype(bf16), (value - high).astype(bf16)


def dot(left, right):
    return jnp.dot(left, right, preferred_element_type=f32)


def dot3(left_high, left_low, right_high, right_low):
    return dot(left_high, right_high) + dot(left_low, right_high) + dot(left_high, right_low)


def cost(flops, bytes_accessed):
    return pl.CostEstimate(flops=int(flops) >> 8, bytes_accessed=int(bytes_accessed) >> 8, transcendentals=0)


def behind(value, *others):
    return value if not others else lax.optimization_barrier((value, others))[0]


def wavenumbers(indices):
    return jnp.where(indices < NV // 2, indices, indices - NV)


def phase_cos_sin(products):
    quarter = NS // 4
    turns = (products + quarter // 2) >> (quarter.bit_length() - 1)
    angle = (products - turns * quarter).astype(f32) * (two_pi / NS)
    square = angle * angle
    cos = 1.0 + square * (-1 / 2 + square * (1 / 24 + square * (-1 / 720 + square * (1 / 40320))))
    sin = 1.0 + square * (
        -1 / 6 + square * (1 / 120 + square * (-1 / 5040 + square * (1 / 362880)))
    )
    sin = sin * angle
    odd = (turns & 1) == 1
    cos, sin = jnp.where(odd, sin, cos), jnp.where(odd, cos, sin)
    turned = turns & 3
    cos = jnp.where((turned == 1) | (turned == 2), -cos, cos)
    sin = jnp.where(turned >= 2, -sin, sin)
    return cos, sin


def table_kernel(parts, starts, cos_high, cos_low, sin_high, sin_low):
    rows, count = cos_high.shape
    step, steps = pl.program_id(0), pl.num_programs(0) // parts
    first = starts[0] if parts == 1 else jnp.where(step < steps, starts[0], starts[1])
    row_ids = first + lax.rem(step, steps) * rows
    row_ids = row_ids + lax.broadcasted_iota(jnp.int32, (rows, LANES), 0)
    lanes = lax.broadcasted_iota(jnp.int32, (rows, LANES), 1)

    cos, sin = phase_cos_sin(row_ids * (starts[2] + lanes))
    step_cos, step_sin = phase_cos_sin(row_ids * LANES)
    for tile in range(count // LANES):
        where = pl.ds(tile * LANES, LANES)
        cos_high[:, where], cos_low[:, where] = split(cos)
        sin_high[:, where], sin_low[:, where] = split(sin)
        cos, sin = cos * step_cos - sin * step_sin, sin * step_cos + cos * step_sin


def phase_table(row_starts, rows, first, count):
    parts = len(row_starts)
    step = math.gcd(rows, 256)
    starts = jnp.stack([jnp.asarray(x, jnp.int32) for x in (row_starts[0], row_starts[-1], first)])
    return pl.pallas_call(
        functools.partial(table_kernel, parts),
        grid=(parts * rows // step,),
        in_specs=[pl.BlockSpec(memory_space=pltpu.SMEM)],
        out_specs=[pl.BlockSpec((step, count), lambda i: (i, 0))] * 4,
        out_shape=[jax.ShapeDtypeStruct((parts * rows, count), bf16)] * 4,
        compiler_params=pltpu.CompilerParams(vmem_limit_bytes=VMEM_MIB * MIB),
        cost_estimate=cost(rows * count * 14, rows * count * 8),
        name="phase_table",
    )(starts)


def merge_kernel(flags, row_ref, col_ref, out_ref):
    rows, cols = out_ref.shape
    from_row, from_col = row_ref[...], col_ref[...]
    upper_home = flags[0] == 1
    plain = jnp.where(upper_home, from_row, from_col)
    mirrored = jnp.where(upper_home, from_col, from_row)

    def flip(size):
        total = lax.broadcasted_iota(jnp.int32, (size, size), 0) + lax.broadcasted_iota(
            jnp.int32, (size, size), 1
        )
        return jnp.where(total == size, 1.0, 0.0).astype(bf16)

    flip_cols, flip_rows = flip(cols), flip(rows)
    high, low = split(mirrored)
    high, low = split(dot(high, flip_cols) + dot(low, flip_cols))
    turned = dot(flip_rows, high) + dot(flip_rows, low)
    out_ref[...] = plain + jnp.where(flags[1] == 1, -turned, turned)


def merge(flags, from_row, from_col):
    rows, cols = from_row.shape
    return pl.pallas_call(
        merge_kernel,
        grid=(1,),
        in_specs=[pl.BlockSpec(memory_space=pltpu.SMEM)]
        + [pl.BlockSpec((rows, cols), lambda i: (0, 0))] * 2,
        out_specs=pl.BlockSpec((rows, cols), lambda i: (0, 0)),
        out_shape=jax.ShapeDtypeStruct((rows, cols), f32),
        compiler_params=pltpu.CompilerParams(vmem_limit_bytes=VMEM_MIB * MIB),
        cost_estimate=cost(4 * rows * cols * (rows + cols), rows * cols * 12),
        name="merge_modes",
    )(flags, from_row, from_col)


def transform_kernel(layout, groups, first, has_base, finish, *refs):
    count = len(layout)
    pieces, refs = refs[:count], refs[count:]
    (turn_cos, turn_sin, c_high, c_low, s_high, s_low), refs = refs[:6], refs[6:]
    if has_base:
        base, refs = refs[:2], refs[2:]
    if finish:
        (yc_high, yc_low, ys_high, ys_low), refs = refs[:4], refs[4:]
    first_out, second_out, modes_high, modes_low = refs
    rows = modes_high.shape[0] // groups

    @pl.when(pl.program_id(0) == 0)
    def _():
        for ref, (group, top) in zip(pieces, layout):
            high, low = split(ref[...])
            where = pl.ds(group * rows + top, ref.shape[0])
            modes_high[where, :] = high
            modes_low[where, :] = low

    high, low = modes_high[...], modes_low[...]
    part_cos = dot3(high, low, c_high[...], c_low[...])
    part_sin = dot3(high, low, s_high[...], s_low[...])
    real, imag = (base[0][...], base[1][...]) if has_base else (None, None)
    for group in range(groups):
        where = slice(group * rows, (group + 1) * rows)
        p = turn_cos[first + group : first + group + 1, :]
        q = turn_sin[first + group : first + group + 1, :]
        more_real = p * part_cos[where] - q * part_sin[where]
        more_imag = p * part_sin[where] + q * part_cos[where]
        real = more_real if real is None else real + more_real
        imag = more_imag if imag is None else imag + more_imag
    if not finish:
        first_out[...] = real
        second_out[...] = imag
        return
    real_high, real_low = split(real)
    imag_high, imag_low = split(imag)
    total = dot3(yc_high[...], yc_low[...], real_high, real_low) - dot3(
        ys_high[...], ys_low[...], imag_high, imag_low
    )
    here = first_out.shape[0]
    first_out[...] = total[:here]
    second_out[...] = total[here:]


def transform(pieces, layout, first, turns, x_tables, y_tables=None, base=None):
    depth, x_count = x_tables[0].shape
    groups = 1 + max(group for group, _ in layout)
    rows = max(top + piece.shape[0] for piece, (_, top) in zip(pieces, layout))
    finish = y_tables is not None
    tile = math.gcd(x_count, 256)
    whole = lambda shape: pl.BlockSpec(shape, lambda i: (0, 0))
    columns = lambda height: pl.BlockSpec((height, tile), lambda i: (0, i))
    flops = 12 * groups * rows * depth * x_count
    out_rows = rows
    operands = [*pieces, *turns, *x_tables]
    specs = [whole(piece.shape) for piece in pieces]
    specs += [columns(turns[0].shape[0])] * 2 + [columns(depth)] * 4
    if base is not None:
        operands += base
        specs += [columns(rows)] * 2
    if finish:
        y_both = y_tables[0].shape[0]
        out_rows = y_both // CORES
        flops += 12 * y_both * rows * x_count
        operands += y_tables
        specs += [whole((y_both, rows))] * 4
    return pl.pallas_call(
        functools.partial(
            transform_kernel, layout, groups, first, base is not None, finish
        ),
        grid=(x_count // tile,),
        in_specs=specs,
        out_specs=[columns(out_rows)] * 2,
        out_shape=[jax.ShapeDtypeStruct((out_rows, x_count), f32)] * 2,
        scratch_shapes=[pltpu.VMEM((groups * rows, depth), bf16)] * 2,
        compiler_params=pltpu.CompilerParams(vmem_limit_bytes=VMEM_MIB * MIB),
        cost_estimate=cost(flops, 12 * MIB),
        name="modes_to_velocity" if finish else "modes_along_x",
    )(*operands)


def stencil_kernel(sign, *refs):
    (centre, before, following, top, bottom, left_edge, right_edge, above, below, flag) = refs[:10]
    velocity = (refs[10:12], refs[12:14], ())
    edge_left, edge_right = refs[14:16]
    acc_out, dz_out = refs[-2:]
    step, steps = pl.program_id(0), pl.num_programs(0)
    s = centre[...]
    rows, cols = s.shape
    row_at = lax.broadcasted_iota(jnp.int32, s.shape, 0)
    col_at = lax.broadcasted_iota(jnp.int32, s.shape, 1)
    back_row = jnp.where(step == 0, top[...], before[before.shape[0] - 1 :, :])
    front_row = jnp.where(step == steps - 1, bottom[...], following[:1, :])
    back = jnp.where(row_at == 0, back_row, pltpu.roll(s, 1, 0))
    front = jnp.where(row_at == rows - 1, front_row, pltpu.roll(s, rows - 1, 0))
    upright = lambda line: jnp.broadcast_to(line, (8, rows)).T[:, :1]
    left = jnp.where(col_at == 0, upright(left_edge[...]), pltpu.roll(s, 1, 1))
    right = jnp.where(col_at == cols - 1, upright(right_edge[...]), pltpu.roll(s, cols - 1, 1))
    up, down = above[...], below[...]
    lap = right + left + front + back + up + down - 6.0 * s
    dz = sign[0].astype(f32) * (up - down)
    transport = None
    for part, diff in enumerate((right - left, front - back, dz)):
        lhs_high, lhs_low = split(edge_left[part].T)
        rhs_high, rhs_low = split(edge_right[part])
        speed = dot3(lhs_high, lhs_low, rhs_high, rhs_low)
        for ref in velocity[part]:
            speed = speed + ref[...]
        transport = speed * diff if transport is None else transport + speed * diff
    acc_out[...] = s - 0.125 * transport + 0.04 * lap - 0.25 * flag[0] * (s - 1.0)
    dz_out[...] = -0.125 * dz


def stencil(sign, scalar, halos, planes, flag_rows, velocity, edges):
    y_count, x_count = scalar.shape
    top, bottom, left_edge, right_edge = halos
    step = BLOCK
    near = 8
    per_step, last = step // near, y_count // near - 1
    rows = pl.BlockSpec((step, x_count), lambda i: (i, 0))
    row = pl.BlockSpec((1, x_count), lambda i: (0, 0))
    column = pl.BlockSpec((1, step), lambda i: (0, i))
    count = edges[0].shape[1]
    return pl.pallas_call(
        stencil_kernel,
        grid=(y_count // step,),
        in_specs=[
            pl.BlockSpec(memory_space=pltpu.SMEM),
            rows,
            pl.BlockSpec((near, x_count), lambda i: (jnp.maximum(i * per_step - 1, 0), 0)),
            pl.BlockSpec((near, x_count), lambda i: (jnp.minimum((i + 1) * per_step, last), 0)),
            row,
            row,
            column,
            column,
            rows,
            rows,
            pl.BlockSpec((1, 1, x_count), lambda i: (i, 0, 0)),
            rows,
            rows,
            rows,
            rows,
            pl.BlockSpec((3, count, step), lambda i: (0, 0, i)),
            pl.BlockSpec((3, count, x_count), lambda i: (0, 0, 0)),
        ],
        out_specs=[rows] * 2,
        out_shape=[jax.ShapeDtypeStruct((y_count, x_count), f32)] * 2,
        compiler_params=pltpu.CompilerParams(vmem_limit_bytes=VMEM_MIB * MIB),
        cost_estimate=cost(30 * y_count * x_count, 40 * y_count * x_count),
        name="stencil",
    )(sign, scalar, scalar, scalar, top, bottom, left_edge, right_edge, *planes, flag_rows, *velocity, *edges)


def ring(array, axis, perm, size):
    arrays = [array]
    for _ in range(size - 1):
        arrays.append(lax.ppermute(arrays[-1], axis, perm))
    return arrays


def edge_factors(edge_rows, edge_cols, x_tables, own_cells, x_cells, y_first):
    upper_rows, col_size, _, _, planes_here, _ = edge_rows.shape
    wave_rows, wave_cols = NV // 2 // upper_rows, NV // col_size
    y_count, x_count = own_cells.shape[0], x_cells.shape[0]
    kept = edge_rows.transpose(2, 4, 0, 3, 1, 5)
    lead = (3, planes_here, upper_rows, 2, col_size)
    high, low = split_outside(kept.reshape(-1, wave_cols))
    part_cos = dot3(high, low, x_tables[0], x_tables[1]).reshape(lead + (x_count,))
    part_sin = dot3(high, low, x_tables[2], x_tables[3]).reshape(lead + (x_count,))
    real = part_cos[:, :, :, 0] - part_sin[:, :, :, 1]
    imag = part_sin[:, :, :, 0] + part_cos[:, :, :, 1]
    block_ids = wavenumbers(jnp.arange(col_size, dtype=jnp.int32) * wave_cols)
    turn_cos, turn_sin = phase_cos_sin(block_ids[:, None] * x_cells[None])
    row_real = jnp.sum(turn_cos * real - turn_sin * imag, axis=3)
    row_imag = jnp.sum(turn_cos * imag + turn_sin * real, axis=3)
    upper_ids = wavenumbers(NV // 2 + jnp.arange(NV // 2, dtype=jnp.int32))
    row_cos, row_sin = phase_cos_sin(upper_ids[::wave_rows, None] * own_cells[None])

    kept = edge_cols.at[..., 0].set(0.0).transpose(2, 4, 3, 1, 0, 5)
    high, low = split_outside(kept.reshape(-1, NV // 2))
    y_tables = phase_table([-NV // 2], NV // 2, y_first, y_count)
    lead = (3, planes_here, 2, col_size, y_count)
    part_cos = dot3(high, low, y_tables[0], y_tables[1]).reshape(lead)
    part_sin = dot3(high, low, y_tables[2], y_tables[3]).reshape(lead)
    col_real = part_cos[:, :, 0] - part_sin[:, :, 1]
    col_imag = part_sin[:, :, 0] + part_cos[:, :, 1]

    spread = lambda array: jnp.broadcast_to(array, (3, planes_here) + array.shape)
    left = jnp.concatenate([spread(row_cos), spread(-row_sin), col_real, -col_imag], axis=2)
    right = jnp.concatenate([row_real, row_imag, spread(turn_cos), spread(turn_sin)], axis=2)
    return left, right


def body(vel_modes, scalar, obstacle):
    planes_here, y_count, x_count = scalar.shape
    wave_rows, wave_cols = vel_modes.shape[3:]
    row_size, col_size = lax.axis_size("row"), lax.axis_size("col")
    row, col = lax.axis_index("row"), lax.axis_index("col")
    pairs = row_size // (2 * CORES)
    upper = row >= row_size // 2
    right = col >= col_size // 2
    mirror = jnp.where(upper, row_size - 1 - row, row)
    batch = [(part, plane) for part in range(3) for plane in range(planes_here)]

    count = len(batch)

    flip_row = [(i, row_size - 1 - i) for i in range(row_size)]
    flip_col = [(i, col_size - 1 - i) for i in range(col_size)]
    next_col = [(i, (i + 1) % col_size) for i in range(col_size)]
    mates = [(i, i // CORES * CORES + (i + 1) % CORES) for i in range(row_size)]
    lower_ring = [
        (i, (i // CORES + 1) % pairs * CORES + i % CORES) for i in range(row_size // 2)
    ]
    next_pair = lower_ring + [(row_size - 1 - i, row_size - 1 - j) for i, j in lower_ring]

    kind = right.astype(jnp.int32)
    flags = jnp.stack([upper.astype(jnp.int32), kind])
    half = wave_rows // 2

    def choose(index, *after):
        part, plane = batch[index]
        modes, which = vel_modes[part, :, plane], behind(kind, *after)
        row_modes = lax.dynamic_index_in_dim(modes, which, 0, keepdims=False)
        col_modes = lax.dynamic_index_in_dim(modes, 1 - which, 0, keepdims=False)
        return row_modes, col_modes

    def meet(chosen, *after):
        row_modes, col_modes = (behind(array, *after) for array in chosen)
        return lax.ppermute(row_modes, "row", flip_row), lax.ppermute(col_modes, "col", flip_col)

    def spread(met, *after):
        own = merge(behind(flags, *after), *met)
        return ring(own, "col", next_col, col_size), lax.ppermute(own, "row", flip_row)

    def relay(index, across, flipped):
        if index < count // 3:
            return [lax.ppermute(piece, "row", flip_row) for piece in across[1:]]
        if index < 2 * (count // 3):
            return ring(flipped, "col", next_col, col_size)[1:]
        top = ring(flipped[:half], "col", next_col, col_size)[1:]
        bottom = [lax.ppermute(piece[half:], "row", flip_row) for piece in across[1:]]
        return [piece for both in zip(top, bottom) for piece in both]

    near_layout = [(group, 0) for group in range(col_size + 1)]
    split_layout = [(group, top) for group in range(col_size - 1) for top in (0, half)]
    whole_layout = [(group, 0) for group in range(col_size - 1)]

    last = count - planes_here
    spreads, relays, sent, kept = [], [], [], []
    first = choose(0)
    met = [meet(first)]

    late_modes, late_scalar = behind(vel_modes, *first), behind(scalar, *first)
    lines = lambda *arrays: jnp.concatenate([array.reshape(-1, LANES) for array in arrays])
    edge_row, edge_col = late_modes[:, :, :, 0, :], late_modes[:, :, :, :, 0]
    message = lines(edge_row, edge_col, late_scalar[:, 0], late_scalar[:, -1])
    second = choose(1, message)
    met.append(meet(second))
    over = lambda i: i + 1 if i % CORES == CORES - 1 else i - 1
    across = [(i, over(i) % row_size) for i in range(row_size)]
    from_across = lax.ppermute(message, "row", across)

    x_first, y_first = col * x_count, row * y_count
    x_cells = x_first + jnp.arange(x_count, dtype=jnp.int32)
    own_cells = y_first + jnp.arange(y_count, dtype=jnp.int32)
    x_tables = phase_table([0], wave_cols, behind(x_first, *second), x_count)
    base_ids, base_shifts = [], []
    for flipped_side in (False, True):
        for step in range(col_size):
            home_col = (col - step) % col_size
            home_upper = upper != flipped_side
            block = jnp.where(home_upper, home_col, col_size - 1 - home_col)
            base_ids.append(wavenumbers(block * wave_cols))
            base_shifts.append((home_col >= col_size // 2).astype(jnp.int32) * (NS // 4))
    base_ids, base_shifts = jnp.stack(base_ids), jnp.stack(base_shifts)
    turns = phase_cos_sin(base_ids[:, None] * x_cells[None] + base_shifts[:, None])

    def gather(index, *after):
        spreads.append(spread(met[index], *after))

    def pass_on(index, *after):
        across, flipped = spreads[index]
        relays.append(relay(index, [behind(x, *after) for x in across], behind(flipped, *after)))

    gather(0, x_tables[0])
    pass_on(0)

    from_across = behind(from_across, *spreads[0][0][1:], spreads[0][1])
    stack, owners = message[None], [list(range(row_size))]
    for stage in range(row_size // CORES):
        perm = across if stage % CORES == 0 else mates
        new = from_across[None] if stage == 0 else lax.ppermute(stack, "row", perm)
        stack = jnp.concatenate([stack, new])
        owners += [[known[sender] for sender, _ in sorted(perm, key=lambda p: p[1])] for known in owners]
    edge_end = (edge_row.size + edge_col.size) // LANES
    side_lines = planes_here * x_count // LANES
    firsts, lasts = stack[:, edge_end : edge_end + side_lines], stack[:, edge_end + side_lines :]
    last_core = row % CORES == CORES - 1
    tops = jnp.where(last_core, lasts[2], lasts[1]).reshape(planes_here, 1, x_count)
    bottoms = jnp.where(last_core, firsts[1], firsts[2]).reshape(planes_here, 1, x_count)
    upper_messages = []
    for place in range(row_size // 2, row_size):
        found = stack[0, :edge_end]
        for item in range(1, stack.shape[0]):
            here = jnp.array([owner == place for owner in owners[item]])[row]
            found = jnp.where(here, stack[item, :edge_end], found)
        upper_messages.append(found)
    message = lines(jnp.stack(upper_messages), late_scalar[:, :, 0], late_scalar[:, :, -1])
    messages = ring(message, "col", next_col, col_size)
    upper_end, side_lines = edge_end * (row_size // 2), planes_here * y_count // LANES
    lefts = messages[1][upper_end + side_lines :].reshape(planes_here, 1, y_count)
    rights = messages[-1][upper_end : upper_end + side_lines].reshape(planes_here, 1, y_count)
    upper_messages = jnp.stack(
        [
            lax.dynamic_index_in_dim(
                jnp.stack(messages), (col - place) % col_size, 0, keepdims=False
            )[:upper_end].reshape(row_size // 2, edge_end, LANES)
            for place in range(col_size)
        ],
        axis=1,
    )

    core = row % CORES
    rows_of = lambda level, i, by: ((level + by) * row_size + i, level * row_size + i)
    one_way, other_way = [], []
    for level in range(lax.axis_size("sec") - 1):
        for i in range(row_size):
            high, low = rows_of(level, i, 1)
            (one_way if i % CORES == 0 else other_way).append((low, high))
            (other_way if i % CORES == 0 else one_way).append((high, low))
    ones = jnp.where(core == 0, scalar[-1:], scalar[:1]) if planes_here > 1 else scalar
    others = jnp.where(core == 0, scalar[:1], scalar[-1:]) if planes_here > 1 else scalar

    mate_first = (row + (row + 1) % CORES - row % CORES) * y_count
    mate_first = behind(mate_first, spreads[0][0][0])
    y_tables = []
    for step in range(pairs):
        rows_block = (mirror // CORES - step) % pairs * CORES + mirror % CORES
        y_tables.append(
            phase_table([mate_first, y_first], y_count, rows_block * wave_rows, wave_rows)
        )
    gather(1, y_tables[-1][0])
    pass_on(1)
    plane_one = lax.ppermute(behind(ones, *spreads[0][0][1:], spreads[0][1]), ("sec", "row"), one_way)

    row_end = edge_row.size // LANES
    lead = (row_size // 2, col_size, 3, 2, planes_here)
    edge_rows = upper_messages[:, :, :row_end].reshape(lead + (wave_cols,))
    edge_cols = upper_messages[:, :, row_end:].reshape(lead + (wave_rows,))
    late = behind(y_first, spreads[1][0][0])
    edge_left, edge_right = edge_factors(edge_rows, edge_cols, x_tables, late + jnp.arange(y_count, dtype=jnp.int32), x_cells, late)
    flag_rows = jnp.repeat(obstacle.astype(f32), BLOCK, axis=2)[:, :, None]

    turns = list(turns)

    def near_part(index, *after):
        across, flipped = spreads[index]
        here = ring_all(across + [flipped])
        turned = [behind(turns[0], *after), turns[1]]
        return [transform(pieces, near_layout, 0, turned, x_tables) for pieces in here]

    def far_part(index, bases, *after):
        send = keep = None
        turned = [behind(turns[0], *after), turns[1]]
        for step, pieces in enumerate(ring_all(relays[index])):
            far_layout = whole_layout if len(pieces) == len(whole_layout) else split_layout
            pair = transform(
                pieces, far_layout, col_size + 1, turned, x_tables, y_tables[step], bases[step]
            )
            send = pair[0] if send is None else send + pair[0]
            keep = pair[1] if keep is None else keep + pair[1]
        kept.append(keep)
        sent.append(lax.ppermute(send, "row", mates))

    def all_parts(index, *after):
        across, flipped = spreads[index]
        layout = near_layout + [(group + col_size + 1, top) for group, top in split_layout]
        send = keep = None
        turned = [behind(turns[0], *after), turns[1]]
        for step, pieces in enumerate(ring_all(across + [flipped] + relays[index])):
            pair = transform(pieces, layout, 0, turned, x_tables, y_tables[step])
            send = pair[0] if send is None else send + pair[0]
            keep = pair[1] if keep is None else keep + pair[1]
        kept.append(keep)
        sent.append(lax.ppermute(send, "row", mates))

    def ring_all(pieces):
        return list(zip(*[ring(piece, "row", next_pair, pairs) for piece in pieces]))

    flat = lambda groups: [array for group in groups for array in group]
    arrived = lambda index: (*spreads[index][0][1:], spreads[index][1])
    chosen = [first, second]
    bases = []
    for index in range(2, count):
        chosen.append(choose(index, *arrived(index - 2)))
        met.append(meet(chosen[index]))
        if index == 2:
            bases.append(near_part(0, spreads[1][0][0], *chosen[2]))
        bases.append(near_part(index - 1, *flat(bases[-1])))
        gather(index, *flat(bases[-1]), *relays[index - 2])
        if index == 2:
            others = behind(others, plane_one, spreads[index][0][0])
            plane_two = lax.ppermute(others, ("sec", "row"), other_way)
        far_part(index - 2, bases[index - 2], spreads[index][0][0])
        pass_on(index, kept[-1])
    far_part(count - 2, bases[-1], kept[-1])
    sides = (edge_left, edge_right, lefts, rights, tops, bottoms, flag_rows)
    first_turn, sides = lax.optimization_barrier((turns[0], sides))
    turns[0] = first_turn
    edge_left, edge_right, lefts, rights, tops, bottoms, flag_rows = sides
    all_parts(count - 1, kept[-1], plane_two)

    sign = 1 - 2 * core
    if planes_here > 1:
        plane_one, plane_two = (
            jnp.where(core == 0, plane_one, plane_two),
            jnp.where(core == 0, plane_two, plane_one),
        )
        sign = jnp.ones_like(sign)
    results = []
    for plane in range(planes_here):
        below = plane_one[0] if plane == 0 else scalar[plane - 1]
        above = plane_two[0] if plane == planes_here - 1 else scalar[plane + 1]
        at = [part * planes_here + plane for part in range(3)]
        acc, factor = stencil(
            sign.reshape(1),
            behind(scalar[plane], kept[at[2]]),
            (tops[plane], bottoms[plane], lefts[plane], rights[plane]),
            (above, below),
            flag_rows[plane],
            [kept[at[0]], sent[at[0]], kept[at[1]], sent[at[1]]],
            (edge_left[:, plane], edge_right[:, plane]),
        )
        results.append(acc + (kept[at[2]] + sent[at[2]]) * factor)
    return jnp.stack(results)


def solution(mesh):
    in_specs = (P(None, None, "sec", "row", "col"), P("sec", "row", "col"), P("sec", "row", "col"))
    out_specs = P("sec", "row", "col")
    return jax.shard_map(body, mesh=mesh, in_specs=in_specs, out_specs=out_specs, check_vma=False)
```
